32 devices in a mesh: rep: 2 (over x), grp: 8 (over z, y), sub: 2 (over core).
Axes of the slice: x: 2, y: 2, z: 4, core: 2. Of those that a mesh axis runs over, the one named last changes fastest.
Arguments:
- trajectory: bfloat16 [24576, 512], P(('rep', 'grp', 'sub')), parts along dimension 0, may hold values from -3 to 3
- text: bfloat16 [24576, 512], P(('rep', 'grp', 'sub')), parts along dimension 0, may hold values from -3 to 3
- instr_ids: int32 [24576], P('rep'), parts along dimension 0, may hold values from 0 to 2047
- plan: int32 [6, 8], P('rep'), parts along dimension 0, may hold values from 0 to 7, as said below
- scale: float32 [1], replicated, may hold values from 2 to 8
- bias: float32 [1], replicated, may hold values from -4 to -1
Outputs:
- loss: float32 [2], P('rep'), parts along dimension 0
- grad_trajectory: float32 [24576, 512], P(('rep', 'grp', 'sub')), parts along dimension 0
- grad_text: float32 [24576, 512], P(('rep', 'grp', 'sub')), parts along dimension 0
The draws below stay inside these ranges and needn't reach their ends.
There are 2 independent parts, one for each index of `rep`. The reference program is written for one: setup_inputs(seed, part) draws one part's arguments, and reference() takes and returns one part's arrays. A program takes and returns all parts, laid end to end along the dimension named above; an argument that names none is the same for every part. Nothing has to cross between parts.
Inputs may be any that keep to these rules, and one draw needn't show every extreme that they name: plan[r, g] = g XOR m_r, where m_r are distinct numbers from 1 to 7, one per round.
All inputs are finite; a program needn't handle non-finite values.
Results may differ from the reference program's by a relative error of at most 0.0003.
The reference program's roundings to bfloat16 on the way count: a program that leaves them out, or rounds other values in their place, can miss the bound.
Values may be sent and summed in bfloat16 or wider, within the bound.
A program may use at most 128 MiB of HBM per device.

```python
import math
import jax
import jax.numpy as jnp
from jax import lax

D = 512
ROUNDS = 3
NIDS = 2048
G = 8
GROUP_ROWS = 1536
B = 12288


def embedding_draw(key, salt):
    key = jax.random.fold_in(key, salt)
    key_scale, key_base = jax.random.split(key, 2)
    scales = jnp.exp(jax.random.uniform(key_scale, (B, 1), jnp.float32, 0.0, math.log(10.0))) * 0.03
    values = jax.random.normal(key_base, (B, D), jnp.float32)
    values = jnp.clip(values, -6.0, 6.0)
    return (values * scales).astype(jnp.bfloat16)


def draw_trajectory(key, part):
    return embedding_draw(key, 11)


def draw_text(key, part):
    return embedding_draw(key, 23)


def draw_plan(key, part):
    key = jax.random.fold_in(key, 37)
    masks = jax.random.permutation(key, G - 1)[:ROUNDS].astype(jnp.int32) + 1
    groups = jnp.arange(G, dtype=jnp.int32)
    return jnp.bitwise_xor(groups[None, :], masks[:, None]).astype(jnp.int32)


def plant(array, own_key, least, top_value):
    longest = array.shape.index(max(array.shape))
    spots = []
    for shift in (0, 1):
        where = [jax.random.randint(jax.random.fold_in(own_key, axis), (), 0, length) for axis, length in enumerate(array.shape)]
        where[longest] = (where[longest] + shift) % array.shape[longest]
        spots.append(tuple(where))
    return array.at[spots[0]].set(least).at[spots[1]].set(top_value)


def setup_inputs(seed: int = 0, part: int = 0) -> dict:
    key_list = jax.random.split(jax.random.key(seed), 7)
    part_splits = jax.random.split(jax.random.fold_in(key_list[6], part), 7)
    return {
        "trajectory": draw_trajectory(jax.random.fold_in(jax.random.fold_in(key_list[6], part), 71), part),
        "text": draw_text(jax.random.fold_in(jax.random.fold_in(key_list[6], part), 71), part),
        "instr_ids": plant(jax.random.randint(part_splits[2], (B,), 0, NIDS), jax.random.fold_in(part_splits[2], 1), 0, NIDS - 1).astype(jnp.int32),
        "plan": draw_plan(jax.random.fold_in(jax.random.fold_in(key_list[6], part), 71), part),
        "scale": jnp.clip(jax.random.uniform(key_list[4], (1,), jnp.float32, 2.0, 8.0), 2.0, 8.0),
        "bias": jnp.clip(jax.random.uniform(key_list[5], (1,), jnp.float32, -4.0, -1.0), -4.0, -1.0),
    }


def normalize(rows):
    values = rows.astype(jnp.float32)
    norm = jnp.sqrt(lax.optimization_barrier(jnp.sum(values * values, axis=1, keepdims=True)) + 1e-06)
    unit = values / norm
    return (unit, unit.astype(jnp.bfloat16), norm)

def block_terms(left, right, left_ids, right_ids, scale, bias):
    sims = lax.dot_general(left, right, (((1,), (1,)), ((), ())), preferred_element_type=jnp.float32)
    signs = jnp.where(left_ids[:, None] == right_ids[None, :], 1.0, -1.0).astype(jnp.float32)
    logits = scale * sims + bias
    terms = jnp.sum(jax.nn.log_sigmoid(signs * logits))
    slopes = (-scale * signs * jax.nn.sigmoid(-signs * logits)).astype(jnp.bfloat16)
    return (terms, slopes)

def finish(unit, norm, grad_unit):
    return (grad_unit - unit * lax.optimization_barrier(jnp.sum(unit * grad_unit, axis=1, keepdims=True))) / norm

def reference(trajectory, text, instr_ids, plan, scale, bias):
    unit_x, low_x, norm_x = normalize(trajectory)
    unit_y, low_y, norm_y = normalize(text)
    xs = low_x.reshape(G, GROUP_ROWS, D)
    ys = low_y.reshape(G, GROUP_ROWS, D)
    ids = instr_ids.reshape(G, GROUP_ROWS)
    linked = jnp.concatenate([jnp.arange(G, dtype=jnp.int32)[None, :], plan.astype(jnp.int32)], axis=0)
    scl = scale[0]
    bs = bias[0]

    def one_group(group):
        grad_x = jnp.zeros((GROUP_ROWS, D), jnp.float32)
        grad_y = jnp.zeros((GROUP_ROWS, D), jnp.float32)
        total = jnp.zeros((), jnp.float32)
        for k in range(1 + ROUNDS):
            other = linked[k, group]
            part, slopes = block_terms(xs[group], ys[other], ids[group], ids[other], scl, bs)
            total = total + part
            grad_x = grad_x + jnp.dot(slopes, ys[other], preferred_element_type=jnp.float32)
            unused, cross = block_terms(xs[other], ys[group], ids[other], ids[group], scl, bs)
            grad_y = grad_y + lax.dot_general(cross, xs[other], (((0,), (0,)), ((), ())), preferred_element_type=jnp.float32)
        return (grad_x, grad_y, total)
    grad_x, grad_y, totals = lax.map(one_group, jnp.arange(G, dtype=jnp.int32))
    loss = (-jnp.sum(totals) / B).reshape(1)
    grad_trajectory = finish(unit_x, norm_x, grad_x.reshape(B, D))
    grad_text = finish(unit_y, norm_y, grad_y.reshape(B, D))
    return (loss, grad_trajectory, grad_text)
```

```python
import functools

import jax
import jax.numpy as jnp
from jax import lax
from jax.experimental import pallas as pl
from jax.experimental.pallas import tpu as pltpu
from jax.sharding import PartitionSpec as P

MESH = pl.DeviceIdType.MESH
LOG2E = 1.4426950408889634
TILE = 256


def ring_position(group, n):
    if n != 8:
        return group
    row, column = group // 2, group % 2
    return row + column * (7 - 2 * row)


def ring_group(position, n):
    if n != 8:
        return position
    column = position // 4
    row = position + column * (7 - 2 * position)
    return 2 * row + column


def kernel(
    n,
    rows,
    linked_ref,
    coef_ref,
    x_ref,
    y_ref,
    own_ids_ref,
    ids_ref,
    grads_ref,
    loss_ref,
    held,
    ring_send,
    ring_recv,
    peer_send,
    peer_recv,
):
    half = n // 2
    group = lax.axis_index("grp")
    sub = lax.axis_index("sub")
    peer = 1 - sub
    pos = ring_position(group, n)
    nexts = (ring_group((pos + 1) % n, n), ring_group((pos + n - 1) % n, n))

    barrier = pltpu.get_barrier_semaphore()
    for target in ({"grp": nexts[0]}, {"grp": nexts[1]}, {"sub": peer}):
        pl.semaphore_signal(barrier, inc=1, device_id=target, device_id_type=MESH)
    pl.semaphore_wait(barrier, 3)

    def ring_copy(way, step, c, kind):
        return pltpu.make_async_remote_copy(
            src_ref=held.at[c, kind, sub],
            dst_ref=held.at[c, kind, sub],
            send_sem=ring_send.at[way, step, kind],
            recv_sem=ring_recv.at[way, step, kind],
            device_id={"grp": nexts[way]},
            device_id_type=MESH,
        )

    def peer_copy(c, kind, side):
        return pltpu.make_async_remote_copy(
            src_ref=held.at[c, kind, side],
            dst_ref=held.at[c, kind, side],
            send_sem=peer_send.at[c, kind],
            recv_sem=peer_recv.at[c, kind],
            device_id={"sub": peer},
            device_id_type=MESH,
        )

    slope_a, slope_b, scale = coef_ref[0], coef_ref[1], coef_ref[2]
    loss_ref[...] = jnp.zeros_like(loss_ref)
    grads_ref[...] = jnp.zeros_like(grads_ref)

    for kind, source in enumerate((x_ref, y_ref)):
        values = source[...].astype(jnp.float32)
        norm = jnp.sqrt(jnp.sum(values * values, axis=1, keepdims=True) + 1e-06)
        held[group, kind, sub] = (values / norm).astype(jnp.bfloat16)
        for way in range(2):
            ring_copy(way, 0, group, kind).start()
        peer_copy(group, kind, sub).start()

    tiles_per_side = rows // TILE
    quarter = rows // 4

    def attend(c, kind):
        weight = linked_ref[c]
        gain = scale * weight

        def tile_step(t, carry):
            side = t // tiles_per_side
            offset = pl.multiple_of((t % tiles_per_side) * TILE, TILE)
            keys = held[c, kind, side, pl.ds(offset, TILE), :]
            queries = held[group, 1 - kind, sub]
            sims = lax.dot_general(
                queries, keys, (((1,), (1,)), ((), ())), preferred_element_type=jnp.float32
            )
            same = own_ids_ref[...] == ids_ref[c * (2 * tiles_per_side) + t]
            e = jnp.exp2(sims * slope_a + slope_b)
            r = 1.0 / (1.0 + e)
            miss = r * jnp.where(same, -1.0, e)
            slopes = (miss * gain).astype(jnp.bfloat16)
            hit = r * jnp.where(same, e, 1.0)
            hits = (hit[:quarter] * hit[quarter : 2 * quarter]) * (
                hit[2 * quarter : 3 * quarter] * hit[3 * quarter :]
            )
            logs = jnp.log(hits).reshape(quarter // 8, 8, TILE)
            loss_ref[kind] += weight * jnp.sum(logs, axis=0)
            grads_ref[1 - kind] += jnp.dot(slopes, keys, preferred_element_type=jnp.float32)
            return carry

        lax.fori_loop(0, 2 * tiles_per_side, tile_step, 0)

    for kind in range(2):
        peer_copy(group, kind, peer).wait_recv()
    for kind in range(2):
        attend(group, kind)

    def event(e, carry):
        k = 1 + e // 2
        kind = e % 2
        cs = (ring_group((pos + n - k) % n, n), ring_group((pos + k) % n, n))
        for way in range(2):
            ring_copy(way, k - 1, cs[way], kind).wait_recv()

            @pl.when(jnp.logical_or(k < half - 1, kind == way))
            def _():
                ring_copy(way, k, cs[way], kind).start()

            peer_copy(cs[way], kind, sub).start()
        for way in range(2):
            peer_copy(cs[way], kind, peer).wait_recv()
            attend(cs[way], kind)
        return carry

    lax.fori_loop(0, 2 * (half - 1), event, 0)

    far = ring_group((pos + half) % n, n)
    for way in range(2):
        ring_copy(way, half - 1, far, way).wait_recv()
        peer_copy(far, way, sub).start()
    for kind in range(2):
        peer_copy(far, kind, peer).wait_recv()
        attend(far, kind)

    def drain(e, carry):
        k = e // 2
        kind = e % 2
        for way in range(2):
            ring_copy(way, k, group, kind).wait_send()
        return carry

    lax.fori_loop(0, 2 * (half - 1), drain, 0)
    for way in range(2):
        ring_copy(way, half - 1, group, way).wait_send()

    def drain_peer(e, carry):
        peer_copy(e // 2, e % 2, sub).wait_send()
        return carry

    lax.fori_loop(0, 2 * n, drain_peer, 0)


def finish(rows, grad_unit):
    values = rows.astype(jnp.float32)
    norm = jnp.sqrt(jnp.sum(values * values, axis=1, keepdims=True) + 1e-06)
    unit = values / norm
    return (grad_unit - unit * jnp.sum(unit * grad_unit, axis=1, keepdims=True)) / norm


def body(n, trajectory, text, instr_ids, plan, scale, bias):
    rows, width = trajectory.shape
    nsub = lax.axis_size("sub")
    group = lax.axis_index("grp")
    sub = lax.axis_index("sub")
    own_ids = lax.dynamic_slice_in_dim(instr_ids, (group * nsub + sub) * rows, rows)
    groups = jnp.arange(n, dtype=jnp.int32)
    links = jnp.logical_or(groups == group, jnp.any(plan[:, group][:, None] == groups[None, :], axis=0))
    coef = jnp.stack([scale[0] * LOG2E, bias[0] * LOG2E, scale[0]])
    half = n // 2
    vmem = pl.BlockSpec(memory_space=pltpu.VMEM)
    smem = pl.BlockSpec(memory_space=pltpu.SMEM)
    pairs = rows * rows * nsub * n * 2
    grads, loss = pl.pallas_call(
        functools.partial(kernel, n, rows),
        out_shape=(
            jax.ShapeDtypeStruct((2, rows, width), jnp.float32),
            jax.ShapeDtypeStruct((2, 8, TILE), jnp.float32),
        ),
        in_specs=[smem, smem, vmem, vmem, vmem, vmem],
        out_specs=(vmem, vmem),
        scratch_shapes=[
            pltpu.VMEM((n, 2, nsub, rows, width), jnp.bfloat16),
            pltpu.SemaphoreType.DMA((2, half, 2)),
            pltpu.SemaphoreType.DMA((2, half, 2)),
            pltpu.SemaphoreType.DMA((n, 2)),
            pltpu.SemaphoreType.DMA((n, 2)),
        ],
        compiler_params=pltpu.CompilerParams(
            collective_id=0, has_side_effects=True, vmem_limit_bytes=62 * 2**20
        ),
        cost_estimate=pl.CostEstimate(
            flops=4 * pairs * width, bytes_accessed=16 * rows * width, transcendentals=3 * pairs
        ),
    )(
        links.astype(jnp.float32),
        coef,
        trajectory,
        text,
        own_ids.reshape(rows, 1),
        instr_ids.reshape(-1, 1, TILE),
    )
    summed = lax.psum(jnp.sum(loss[1]), ("grp", "sub"))
    total = (-summed / (rows * nsub * n)).reshape(1)
    return (total, finish(trajectory, grads[0]), finish(text, grads[1]))


def solution(mesh):
    n = mesh.shape["grp"]
    return jax.shard_map(
        functools.partial(body, n),
        mesh=mesh,
        in_specs=(
            P(("rep", "grp", "sub"), None),
            P(("rep", "grp", "sub"), None),
            P("rep"),
            P("rep", None),
            P(),
            P(),
        ),
        out_specs=(P("rep"), P(("rep", "grp", "sub"), None), P(("rep", "grp", "sub"), None)),
        check_vma=False,
    )
```

```python
import functools

import jax
import jax.numpy as jnp
from jax import lax
from jax.experimental import pallas as pl
from jax.experimental.pallas import tpu as pltpu
from jax.sharding import PartitionSpec as P

MESH = pl.DeviceIdType.MESH
LOG2E = 1.4426950408889634
TILE = 256
BLOCK = 64
UNROLL = 2


def ring_position(group, n):
    if n != 8:
        return group
    row, column = group // 2, group % 2
    return row + column * (7 - 2 * row)


def ring_group(position, n):
    if n != 8:
        return position
    column = position // 4
    row = position + column * (7 - 2 * position)
    return 2 * row + column


def kernel(
    n,
    rows,
    linked_ref,
    coef_ref,
    x_ref,
    y_ref,
    own_ids_ref,
    ids_ref,
    loss_out,
    grad_x_ref,
    grad_y_ref,
    held,
    grads_ref,
    loss_ref,
    shares,
    ring_send,
    ring_recv,
    peer_send,
    peer_recv,
    far_send,
    far_recv,
    share_send,
    share_recv,
):
    half = n // 2
    group = lax.axis_index("grp")
    sub = lax.axis_index("sub")
    peer = 1 - sub
    pos = ring_position(group, n)
    nexts = (ring_group((pos + 1) % n, n), ring_group((pos + n - 1) % n, n))

    me = group * 2 + sub

    def at_offset(d):
        other = (me + d) % (2 * n)
        return {"grp": other // 2, "sub": other % 2}

    barrier = pltpu.get_barrier_semaphore()

    def greet(d, carry):
        pl.semaphore_signal(barrier, inc=1, device_id=at_offset(d), device_id_type=MESH)
        return carry

    lax.fori_loop(1, 2 * n, greet, 0)
    pl.semaphore_wait(barrier, 2 * n - 1)

    def ring_copy(way, step, c, kind):
        return pltpu.make_async_remote_copy(
            src_ref=held.at[c, kind, sub],
            dst_ref=held.at[c, kind, sub],
            send_sem=ring_send.at[way, step, kind],
            recv_sem=ring_recv.at[way, step, kind],
            device_id={"grp": nexts[way]},
            device_id_type=MESH,
        )

    def peer_copy(c, kind, side):
        return pltpu.make_async_remote_copy(
            src_ref=held.at[c, kind, side],
            dst_ref=held.at[c, kind, side],
            send_sem=peer_send.at[c, kind],
            recv_sem=peer_recv.at[c, kind],
            device_id={"sub": peer},
            device_id_type=MESH,
        )

    def far_copy(way, c, kind, part):
        piece = held.at[c, kind, sub, pl.ds(part * TILE, TILE)]
        return pltpu.make_async_remote_copy(
            src_ref=piece,
            dst_ref=piece,
            send_sem=far_send.at[way, part],
            recv_sem=far_recv.at[way, part],
            device_id={"grp": nexts[way]},
            device_id_type=MESH,
        )

    def far_peer_copy(c, kind, side, part):
        piece = held.at[c, kind, side, pl.ds(part * TILE, TILE)]
        return pltpu.make_async_remote_copy(
            src_ref=piece,
            dst_ref=piece,
            send_sem=far_send.at[2 + kind, part],
            recv_sem=far_recv.at[2 + kind, part],
            device_id={"sub": peer},
            device_id_type=MESH,
        )

    def share_copy(d, slot):
        return pltpu.make_async_remote_copy(
            src_ref=shares.at[slot],
            dst_ref=shares.at[slot],
            send_sem=share_send.at[d],
            recv_sem=share_recv.at[d],
            device_id=at_offset(d),
            device_id_type=MESH,
        )

    slope_a, slope_b, scale = coef_ref[0], coef_ref[1], coef_ref[2]
    loss_ref[...] = jnp.zeros_like(loss_ref)
    grads_ref[...] = jnp.zeros_like(grads_ref)

    for kind, source in enumerate((x_ref, y_ref)):
        values = source[...].astype(jnp.float32)
        norm = jnp.sqrt(jnp.sum(values * values, axis=1, keepdims=True) + 1e-06)
        held[group, kind, sub] = (values / norm).astype(jnp.bfloat16)
        for way in range(2):
            ring_copy(way, 0, group, kind).start()
        peer_copy(group, kind, sub).start()

    tiles_per_side = rows // TILE
    quarter = rows // 4

    def attend_tile(c, kind, side, tile):
        weight = linked_ref[c]
        gain = scale * weight
        offset = pl.multiple_of(tile * TILE, TILE)
        keys = held[c, kind, side, pl.ds(offset, TILE), :]
        queries = held[group, 1 - kind, sub]
        sims = lax.dot_general(
            queries, keys, (((1,), (1,)), ((), ())), preferred_element_type=jnp.float32
        )
        same = own_ids_ref[...] == ids_ref[(c * 2 + side) * tiles_per_side + tile]
        e = jnp.exp2(sims * slope_a + slope_b)
        r = 1.0 / (1.0 + e)
        miss = r * jnp.where(same, -1.0, e)
        slopes = (miss * gain).astype(jnp.bfloat16)
        hit = r * jnp.where(same, e, 1.0)
        hits = (hit[:quarter] * hit[quarter : 2 * quarter]) * (
            hit[2 * quarter : 3 * quarter] * hit[3 * quarter :]
        )
        logs = jnp.log(hits).reshape(quarter // 8, 8, TILE)
        loss_ref[kind] += weight * jnp.sum(logs, axis=0)
        grads_ref[1 - kind] += jnp.dot(slopes, keys, preferred_element_type=jnp.float32)

    def attend(c, kind):
        def tile_step(t, carry):
            attend_tile(c, kind, t // tiles_per_side, t % tiles_per_side)
            return carry

        lax.fori_loop(0, 2 * tiles_per_side, tile_step, 0, unroll=UNROLL)

    def finish(kind, rows_ref, out_ref):
        def block(i, carry):
            at = pl.ds(pl.multiple_of(i * BLOCK, BLOCK), BLOCK)
            values = rows_ref[at, :].astype(jnp.float32)
            norm = jnp.sqrt(jnp.sum(values * values, axis=1, keepdims=True) + 1e-06)
            unit = values / norm
            grad = grads_ref[kind, at, :]
            along = jnp.sum(unit * grad, axis=1, keepdims=True)
            out_ref[at, :] = (grad - unit * along) / norm
            return carry

        lax.fori_loop(0, rows // BLOCK, block, 0)

    for kind in range(2):
        peer_copy(group, kind, peer).wait_recv()
    for kind in range(2):
        attend(group, kind)

    def event(e, carry):
        k = 1 + e // 2
        kind = e % 2
        cs = (ring_group((pos + n - k) % n, n), ring_group((pos + k) % n, n))
        for way in range(2):
            ring_copy(way, k - 1, cs[way], kind).wait_recv()

            @pl.when(k < half - 1)
            def _():
                ring_copy(way, k, cs[way], kind).start()

            @pl.when(jnp.logical_and(k == half - 1, kind == way))
            def _():
                for part in range(tiles_per_side):
                    far_copy(way, cs[way], way, part).start()

            peer_copy(cs[way], kind, sub).start()
        for way in range(2):
            peer_copy(cs[way], kind, peer).wait_recv()
            attend(cs[way], kind)
        return carry

    lax.fori_loop(0, 2 * (half - 1), event, 0)

    far = ring_group((pos + half) % n, n)
    for part in range(tiles_per_side):
        for way in range(2):
            far_copy(way, far, way, part).wait_recv()
            far_peer_copy(far, way, sub, part).start()
        attend_tile(far, 1, sub, part)
        attend_tile(far, 0, sub, part)
        for kind in range(2):
            far_peer_copy(far, kind, peer, part).wait_recv()
        attend_tile(far, 1, peer, part)
        if part == tiles_per_side - 1:
            partial = loss_ref[1]
            shares[me] = partial[:, :128] + partial[:, 128:]

            def share(d, carry):
                share_copy(d, me).start()
                return carry

            lax.fori_loop(1, 2 * n, share, 0)
        attend_tile(far, 0, peer, part)

    finish(0, x_ref, grad_x_ref)
    finish(1, y_ref, grad_y_ref)

    def drain(e, carry):
        k = e // 2
        kind = e % 2
        for way in range(2):
            ring_copy(way, k, group, kind).wait_send()
        return carry

    lax.fori_loop(0, 2 * (half - 1), drain, 0)

    def drain_peer(e, carry):
        peer_copy((far + 1 + e // 2) % n, e % 2, sub).wait_send()
        return carry

    lax.fori_loop(0, 2 * (n - 1), drain_peer, 0)
    for part in range(tiles_per_side):
        for kind in range(2):
            far_copy(kind, far, kind, part).wait_send()
            far_peer_copy(far, kind, sub, part).wait_send()

    def collect(d, carry):
        share_copy(d, (me + 2 * n - d) % (2 * n)).wait_recv()
        share_copy(d, me).wait_send()
        return carry

    lax.fori_loop(1, 2 * n, collect, 0)
    summed = jnp.sum(jnp.sum(shares[...], axis=0))
    loss_out[0] = -summed / (2 * n * rows)


def body(n, trajectory, text, instr_ids, plan, scale, bias):
    rows, width = trajectory.shape
    nsub = lax.axis_size("sub")
    group = lax.axis_index("grp")
    sub = lax.axis_index("sub")
    own_ids = lax.dynamic_slice_in_dim(instr_ids, (group * nsub + sub) * rows, rows)
    groups = jnp.arange(n, dtype=jnp.int32)
    links = jnp.logical_or(groups == group, jnp.any(plan[:, group][:, None] == groups[None, :], axis=0))
    coef = jnp.stack([scale[0] * LOG2E, bias[0] * LOG2E, scale[0]])
    half = n // 2
    vmem = pl.BlockSpec(memory_space=pltpu.VMEM)
    smem = pl.BlockSpec(memory_space=pltpu.SMEM)
    pairs = rows * rows * nsub * n * 2
    return pl.pallas_call(
        functools.partial(kernel, n, rows),
        out_shape=(
            jax.ShapeDtypeStruct((1,), jnp.float32),
            jax.ShapeDtypeStruct((rows, width), jnp.float32),
            jax.ShapeDtypeStruct((rows, width), jnp.float32),
        ),
        in_specs=[smem, smem, vmem, vmem, vmem, vmem],
        out_specs=(smem, vmem, vmem),
        scratch_shapes=[
            pltpu.VMEM((n, 2, nsub, rows, width), jnp.bfloat16),
            pltpu.VMEM((2, rows, width), jnp.float32),
            pltpu.VMEM((2, 8, TILE), jnp.float32),
            pltpu.VMEM((2 * n, 8, 128), jnp.float32),
            pltpu.SemaphoreType.DMA((2, half, 2)),
            pltpu.SemaphoreType.DMA((2, half, 2)),
            pltpu.SemaphoreType.DMA((n, 2)),
            pltpu.SemaphoreType.DMA((n, 2)),
            pltpu.SemaphoreType.DMA((4, rows // TILE)),
            pltpu.SemaphoreType.DMA((4, rows // TILE)),
            pltpu.SemaphoreType.DMA((2 * n,)),
            pltpu.SemaphoreType.DMA((2 * n,)),
        ],
        compiler_params=pltpu.CompilerParams(
            collective_id=0, has_side_effects=True, vmem_limit_bytes=62 * 2**20
        ),
        cost_estimate=pl.CostEstimate(
            flops=4 * pairs * width, bytes_accessed=16 * rows * width, transcendentals=3 * pairs
        ),
    )(
        links.astype(jnp.float32),
        coef,
        trajectory,
        text,
        own_ids.reshape(rows, 1),
        instr_ids.reshape(-1, 1, TILE),
    )


def solution(mesh):
    n = mesh.shape["grp"]
    return jax.shard_map(
        functools.partial(body, n),
        mesh=mesh,
        in_specs=(
            P(("rep", "grp", "sub"), None),
            P(("rep", "grp", "sub"), None),
            P("rep"),
            P("rep", None),
            P(),
            P(),
        ),
        out_specs=(P("rep"), P(("rep", "grp", "sub"), None), P(("rep", "grp", "sub"), None)),
        check_vma=False,
    )
```

```python
import functools

import jax
import jax.numpy as jnp
from jax import lax
from jax.experimental import pallas as pl
from jax.experimental.pallas import tpu as pltpu
from jax.sharding import PartitionSpec as P

MESH = pl.DeviceIdType.MESH
LOG2E = 1.4426950408889634
TILE = 256
BLOCK = 64
UNROLL = 2


def ring_position(group, n):
    if n != 8:
        return group
    row, column = group // 2, group % 2
    return row + column * (7 - 2 * row)


def ring_group(position, n):
    if n != 8:
        return position
    column = position // 4
    row = position + column * (7 - 2 * position)
    return 2 * row + column


def kernel(
    n,
    rows,
    plan_ref,
    scale_ref,
    bias_ref,
    x_ref,
    y_ref,
    own_ids_ref,
    ids_ref,
    loss_out,
    grad_x_ref,
    grad_y_ref,
    held,
    grads_ref,
    loss_ref,
    shares,
    ring_send,
    ring_recv,
    peer_send,
    peer_recv,
    far_send,
    far_recv,
    share_send,
    share_recv,
):
    half = n // 2
    group = lax.axis_index("grp")
    sub = lax.axis_index("sub")
    peer = 1 - sub
    pos = ring_position(group, n)
    nexts = (ring_group((pos + 1) % n, n), ring_group((pos + n - 1) % n, n))

    me = group * 2 + sub

    def at_offset(d):
        other = (me + d) % (2 * n)
        return {"grp": other // 2, "sub": other % 2}

    barrier = pltpu.get_barrier_semaphore()

    def greet(d, carry):
        pl.semaphore_signal(barrier, inc=1, device_id=at_offset(d), device_id_type=MESH)
        return carry

    lax.fori_loop(1, 2 * n, greet, 0)

    def ring_copy(way, step, c, kind):
        return pltpu.make_async_remote_copy(
            src_ref=held.at[c, kind, sub],
            dst_ref=held.at[c, kind, sub],
            send_sem=ring_send.at[way, step, kind],
            recv_sem=ring_recv.at[way, step, kind],
            device_id={"grp": nexts[way]},
            device_id_type=MESH,
        )

    def peer_copy(c, kind, side):
        return pltpu.make_async_remote_copy(
            src_ref=held.at[c, kind, side],
            dst_ref=held.at[c, kind, side],
            send_sem=peer_send.at[c, kind],
            recv_sem=peer_recv.at[c, kind],
            device_id={"sub": peer},
            device_id_type=MESH,
        )

    def far_copy(way, c, kind, part):
        piece = held.at[c, kind, sub, pl.ds(part * TILE, TILE)]
        return pltpu.make_async_remote_copy(
            src_ref=piece,
            dst_ref=piece,
            send_sem=far_send.at[way, part],
            recv_sem=far_recv.at[way, part],
            device_id={"grp": nexts[way]},
            device_id_type=MESH,
        )

    def far_peer_copy(c, kind, side, part):
        piece = held.at[c, kind, side, pl.ds(part * TILE, TILE)]
        return pltpu.make_async_remote_copy(
            src_ref=piece,
            dst_ref=piece,
            send_sem=far_send.at[2 + kind, part],
            recv_sem=far_recv.at[2 + kind, part],
            device_id={"sub": peer},
            device_id_type=MESH,
        )

    def share_copy(d, slot):
        return pltpu.make_async_remote_copy(
            src_ref=shares.at[slot],
            dst_ref=shares.at[slot],
            send_sem=share_send.at[d],
            recv_sem=share_recv.at[d],
            device_id=at_offset(d),
            device_id_type=MESH,
        )

    scale = scale_ref[0]
    slope_a, slope_b = scale * LOG2E, bias_ref[0] * LOG2E
    partners = [plan_ref[r, group] for r in range(plan_ref.shape[0])]

    def normalize(kind, source):
        values = source[...].astype(jnp.float32)
        norm = jnp.sqrt(jnp.sum(values * values, axis=1, keepdims=True) + 1e-06)
        held[group, kind, sub] = (values / norm).astype(jnp.bfloat16)

    normalize(0, x_ref)
    pl.semaphore_wait(barrier, 2 * n - 1)
    for way in range(2):
        ring_copy(way, 0, group, 0).start()
    peer_copy(group, 0, sub).start()
    normalize(1, y_ref)
    for way in range(2):
        ring_copy(way, 0, group, 1).start()
    peer_copy(group, 1, sub).start()
    loss_ref[...] = jnp.zeros_like(loss_ref)
    grads_ref[...] = jnp.zeros_like(grads_ref)

    tiles_per_side = rows // TILE
    quarter = rows // 4

    def attend_tile(c, kind, side, tile):
        weight = jnp.where(c == group, 1.0, 0.0)
        for partner in partners:
            weight = jnp.where(c == partner, 1.0, weight)
        gain = scale * weight
        offset = pl.multiple_of(tile * TILE, TILE)
        keys = held[c, kind, side, pl.ds(offset, TILE), :]
        queries = held[group, 1 - kind, sub]
        sims = lax.dot_general(
            queries, keys, (((1,), (1,)), ((), ())), preferred_element_type=jnp.float32
        )
        same = own_ids_ref[...] == ids_ref[(c * 2 + side) * tiles_per_side + tile]
        e = jnp.exp2(sims * slope_a + slope_b)
        r = 1.0 / (1.0 + e)
        miss = r * jnp.where(same, -1.0, e)
        slopes = (miss * gain).astype(jnp.bfloat16)
        hit = r * jnp.where(same, e, 1.0)
        hits = (hit[:quarter] * hit[quarter : 2 * quarter]) * (
            hit[2 * quarter : 3 * quarter] * hit[3 * quarter :]
        )
        logs = jnp.log(hits).reshape(quarter // 8, 8, TILE)
        loss_ref[kind] += weight * jnp.sum(logs, axis=0)
        grads_ref[1 - kind] += jnp.dot(slopes, keys, preferred_element_type=jnp.float32)

    def attend(c, kind):
        def tile_step(t, carry):
            attend_tile(c, kind, t // tiles_per_side, t % tiles_per_side)
            return carry

        lax.fori_loop(0, 2 * tiles_per_side, tile_step, 0, unroll=UNROLL)

    def finish(kind, rows_ref, out_ref):
        def block(i, carry):
            at = pl.ds(pl.multiple_of(i * BLOCK, BLOCK), BLOCK)
            values = rows_ref[at, :].astype(jnp.float32)
            norm = jnp.sqrt(jnp.sum(values * values, axis=1, keepdims=True) + 1e-06)
            unit = values / norm
            grad = grads_ref[kind, at, :]
            along = jnp.sum(unit * grad, axis=1, keepdims=True)
            out_ref[at, :] = (grad - unit * along) / norm
            return carry

        lax.fori_loop(0, rows // BLOCK, block, 0)

    for kind in range(2):
        peer_copy(group, kind, peer).wait_recv()
    attend(group, 0)
    attend(group, 1)

    def event(e, carry):
        k = 1 + e // 2
        kind = e % 2
        cs = (ring_group((pos + n - k) % n, n), ring_group((pos + k) % n, n))
        for way in range(2):
            ring_copy(way, k - 1, cs[way], kind).wait_recv()

            @pl.when(k < half - 1)
            def _():
                ring_copy(way, k, cs[way], kind).start()

            @pl.when(jnp.logical_and(k == half - 1, kind == way))
            def _():
                for part in range(tiles_per_side):
                    far_copy(way, cs[way], way, part).start()

            peer_copy(cs[way], kind, sub).start()
        for way in range(2):
            peer_copy(cs[way], kind, peer).wait_recv()
            attend(cs[way], kind)
        return carry

    lax.fori_loop(0, 2 * (half - 1), event, 0)

    far = ring_group((pos + half) % n, n)
    for part in range(tiles_per_side):
        for way in range(2):
            far_copy(way, far, way, part).wait_recv()
            far_peer_copy(far, way, sub, part).start()
        attend_tile(far, 1, sub, part)
        attend_tile(far, 0, sub, part)
        for kind in range(2):
            far_peer_copy(far, kind, peer, part).wait_recv()
        attend_tile(far, 1, peer, part)
        if part == tiles_per_side - 1:
            partial = loss_ref[1]
            shares[me] = partial[:, :128] + partial[:, 128:]

            def share(d, carry):
                share_copy(d, me).start()
                return carry

            lax.fori_loop(1, 2 * n, share, 0)
        attend_tile(far, 0, peer, part)

    finish(0, x_ref, grad_x_ref)
    finish(1, y_ref, grad_y_ref)

    def drain(e, carry):
        k = e // 2
        kind = e % 2
        for way in range(2):
            ring_copy(way, k, group, kind).wait_send()
        return carry

    lax.fori_loop(0, 2 * (half - 1), drain, 0)

    def drain_peer(e, carry):
        peer_copy((far + 1 + e // 2) % n, e % 2, sub).wait_send()
        return carry

    lax.fori_loop(0, 2 * (n - 1), drain_peer, 0)
    for part in range(tiles_per_side):
        for kind in range(2):
            far_copy(kind, far, kind, part).wait_send()
            far_peer_copy(far, kind, sub, part).wait_send()

    def collect(d, carry):
        share_copy(d, (me + 2 * n - d) % (2 * n)).wait_recv()
        share_copy(d, me).wait_send()
        return carry

    lax.fori_loop(1, 2 * n, collect, 0)
    summed = jnp.sum(jnp.sum(shares[...], axis=0))
    loss_out[0] = -summed / (2 * n * rows)


def body(n, trajectory, text, instr_ids, plan, scale, bias):
    rows, width = trajectory.shape
    nsub = lax.axis_size("sub")
    group = lax.axis_index("grp")
    sub = lax.axis_index("sub")
    own_ids = lax.dynamic_slice_in_dim(instr_ids, (group * nsub + sub) * rows, rows)
    half = n // 2
    vmem = pl.BlockSpec(memory_space=pltpu.VMEM)
    smem = pl.BlockSpec(memory_space=pltpu.SMEM)
    pairs = rows * rows * nsub * n * 2
    return pl.pallas_call(
        functools.partial(kernel, n, rows),
        out_shape=(
            jax.ShapeDtypeStruct((1,), jnp.float32),
            jax.ShapeDtypeStruct((rows, width), jnp.float32),
            jax.ShapeDtypeStruct((rows, width), jnp.float32),
        ),
        in_specs=[smem, smem, smem, vmem, vmem, vmem, vmem],
        out_specs=(smem, vmem, vmem),
        scratch_shapes=[
            pltpu.VMEM((n, 2, nsub, rows, width), jnp.bfloat16),
            pltpu.VMEM((2, rows, width), jnp.float32),
            pltpu.VMEM((2, 8, TILE), jnp.float32),
            pltpu.VMEM((2 * n, 8, 128), jnp.float32),
            pltpu.SemaphoreType.DMA((2, half, 2)),
            pltpu.SemaphoreType.DMA((2, half, 2)),
            pltpu.SemaphoreType.DMA((n, 2)),
            pltpu.SemaphoreType.DMA((n, 2)),
            pltpu.SemaphoreType.DMA((4, rows // TILE)),
            pltpu.SemaphoreType.DMA((4, rows // TILE)),
            pltpu.SemaphoreType.DMA((2 * n,)),
            pltpu.SemaphoreType.DMA((2 * n,)),
        ],
        compiler_params=pltpu.CompilerParams(
            collective_id=0, has_side_effects=True, vmem_limit_bytes=62 * 2**20
        ),
        cost_estimate=pl.CostEstimate(
            flops=4 * pairs * width, bytes_accessed=16 * rows * width, transcendentals=3 * pairs
        ),
    )(
        plan,
        scale,
        bias,
        trajectory,
        text,
        own_ids.reshape(rows, 1),
        instr_ids.reshape(-1, 1, TILE),
    )


def solution(mesh):
    n = mesh.shape["grp"]
    return jax.shard_map(
        functools.partial(body, n),
        mesh=mesh,
        in_specs=(
            P(("rep", "grp", "sub"), None),
            P(("rep", "grp", "sub"), None),
            P("rep"),
            P("rep", None),
            P(),
            P(),
        ),
        out_specs=(P("rep"), P(("rep", "grp", "sub"), None), P(("rep", "grp", "sub"), None)),
        check_vma=False,
    )
```
